256 devices in a mesh: seg: 16 (over y, x), ctx: 16 (over z, core).
Axes of the slice: x: 4, y: 4, z: 8, core: 2. Of those that a mesh axis runs over, the one named last changes fastest.
Arguments:
- queries: bfloat16 [393216, 1024], P(('seg', 'ctx')), may hold values from -6 to 6
- keys: bfloat16 [393216, 1024], P(('seg', 'ctx')), may hold values from -6 to 6
- values: bfloat16 [393216, 1024], P(('seg', 'ctx')), may hold values from -6 to 6
- log_decay: float32 [8, 393216], P(None, ('seg', 'ctx')), may hold values from -1 to 0, as said below
- gain: float32 [1024], replicated, may hold values from 0.1 to 1.9
Outputs:
- attended: bfloat16 [393216, 1024], P(('seg', 'ctx'))
The draws below stay inside these ranges and needn't reach their ends.
Inputs may be any that keep to these rules, and one draw needn't show every extreme that they name: `log_decay`: every entry is negative.
All inputs are finite; a program needn't handle non-finite values.
Results may differ from the reference program's by a relative error of at most 0.0039.
Values sent between devices are 32-bit elements; how exact they have to be, the bound alone decides.
A program may use at most 320 MiB of HBM per device.

```python
import jax
import jax.numpy as jnp
from jax import lax

HEADS_PER_BATCH = 8
HD = 128
BLOCK = 512
TOK_DEV = 1536
SEQUENCE_SPAN = 393216


def token_levels(key):
    count = SEQUENCE_SPAN // BLOCK
    place = (jnp.arange(count, dtype=jnp.float32) + 0.5) / count
    jitter = jax.random.uniform(key, (count,), jnp.float32, -0.5, 0.5)
    return jnp.repeat(jnp.exp(0.5 - 4.0 * place + jitter), BLOCK)


def draw_keys(key, part):
    key = jax.random.fold_in(key, 11)
    key_base, key_level = jax.random.split(key, 2)
    shape = (SEQUENCE_SPAN, HEADS_PER_BATCH * HD)
    base = jax.random.truncated_normal(key_base, -6.0, 6.0, shape, jnp.float32)
    levels = token_levels(key_level)
    return jnp.clip(base * levels[:, None], -6.0, 6.0).astype(jnp.bfloat16)


def draw_values(key, part):
    key = jax.random.fold_in(key, 13)
    key_base, key_level = jax.random.split(key, 2)
    shape = (SEQUENCE_SPAN, HEADS_PER_BATCH * HD)
    base = jax.random.truncated_normal(key_base, -6.0, 6.0, shape, jnp.float32)
    levels = token_levels(key_level)
    return jnp.clip(base * levels[:, None], -6.0, 6.0).astype(jnp.bfloat16)


def draw_log_decay(key, part):
    key = jax.random.fold_in(key, 7)
    key_pick, key_fast, key_slow, random_seed_scaling, key_where, random_seed_fading = jax.random.split(key, 6)
    quick_count = max(1, HEADS_PER_BATCH // 2)
    order = jax.random.permutation(key_pick, HEADS_PER_BATCH)
    quick = order < quick_count
    fast_rate = jnp.exp(jax.random.uniform(key_fast, (HEADS_PER_BATCH,), jnp.float32, jnp.log(0.03 / TOK_DEV), jnp.log(0.08 / TOK_DEV)))
    slow_rate = 0.4 / SEQUENCE_SPAN * jnp.exp(jax.random.uniform(key_slow, (HEADS_PER_BATCH,), jnp.float32, jnp.log(0.5), 0.0))
    shrink_speed = jnp.where(quick, fast_rate, slow_rate)
    shrink_multiplier = jnp.exp(jax.random.uniform(random_seed_scaling, (SEQUENCE_SPAN // BLOCK,), jnp.float32, jnp.log(0.6), jnp.log(1.6)))
    shrink_multiplier = jnp.repeat(shrink_multiplier, BLOCK)
    locations = jax.random.randint(key_where, (2,), 0, SEQUENCE_SPAN)
    fading_logits = jax.random.uniform(random_seed_fading, (2, HEADS_PER_BATCH), jnp.float32, 0.2, 0.5)
    offset_along = jnp.arange(SEQUENCE_SPAN)
    wipe_event = jnp.zeros((HEADS_PER_BATCH, SEQUENCE_SPAN), jnp.float32)
    for event_position in range(2):
        event_chooser = (offset_along == locations[event_position])[None, :]
        wipe_event = wipe_event + jnp.where(event_chooser, jnp.log(1.0 - fading_logits[event_position])[:, None], 0.0)
    return -(shrink_speed[:, None] * shrink_multiplier[None, :]) + wipe_event


def steps_of(own_key, dims, cuts, smallest, top_value):
    level = 1.0
    for position, shards_of in cuts:
        heights = jax.random.uniform(jax.random.fold_in(jax.random.fold_in(own_key, 6), position), (shards_of,), jnp.float32, smallest / len(cuts), top_value / len(cuts))
        level = level * jnp.repeat(jnp.exp(heights), dims[position] // shards_of).reshape((-1,) + (1,) * (len(dims) - 1 - position))
    return level


def bell_draw(stream_key, shape, width, most, cuts=(), kind=jnp.bfloat16):
    values = width * jax.random.normal(stream_key, shape, jnp.float32)
    if cuts:
        values = values * steps_of(stream_key, shape, cuts, -0.22, 0.18)
    return jnp.clip(values, -most, most).astype(kind)


def setup_inputs(seed: int = 0) -> dict:
    streams_of = jax.random.split(jax.random.key(seed), 6)
    return {
        "queries": bell_draw(streams_of[0], (SEQUENCE_SPAN, HEADS_PER_BATCH * HD), 1.0, 6.0, ((0, 256),)),
        "keys": draw_keys(jax.random.fold_in(streams_of[5], 71), 0),
        "values": draw_values(jax.random.fold_in(streams_of[5], 71), 0),
        "log_decay": draw_log_decay(jax.random.fold_in(streams_of[5], 71), 0),
        "gain": jnp.clip(1.0 + 0.18 * jax.random.normal(streams_of[4], (HEADS_PER_BATCH * HD,), jnp.float32), 0.1, 1.9),
    }


def block_step(state, queries, keys, values, decay):
    cum = jnp.cumsum(decay, axis=1)
    size = decay.shape[1]
    rows = lax.broadcasted_iota(jnp.int32, (size, size), 0)
    cols = lax.broadcasted_iota(jnp.int32, (size, size), 1)
    below = (cols <= rows)[None]
    scores = jnp.einsum('thd,shd->hts', queries, keys, preferred_element_type=jnp.float32)
    spread = jnp.where(below, cum[:, :, None] - cum[:, None, :], 0.0)
    weights = jnp.where(below, jnp.exp(spread), 0.0) * scores
    weights = weights.astype(jnp.bfloat16)
    inside = jnp.einsum('hts,shd->thd', weights, values, preferred_element_type=jnp.float32)
    scaled = queries.astype(jnp.float32) * jnp.exp(cum).T[:, :, None]
    inside = inside + jnp.einsum('thd,hde->the', scaled, state, precision=lax.Precision.HIGHEST)
    last = cum[:, -1]
    decayed_keys = (keys.astype(jnp.float32) * jnp.exp(last[:, None] - cum).T[:, :, None]).astype(jnp.bfloat16)
    added = jnp.einsum('shd,she->hde', decayed_keys, values, preferred_element_type=jnp.float32)
    state = jnp.exp(last)[:, None, None] * state + added
    return (state, inside)

def reference(queries, keys, values, log_decay, gain):
    count = SEQUENCE_SPAN // BLOCK
    q_blocks = queries.reshape(count, BLOCK, HEADS_PER_BATCH, HD)
    k_blocks = keys.reshape(count, BLOCK, HEADS_PER_BATCH, HD)
    v_blocks = values.reshape(count, BLOCK, HEADS_PER_BATCH, HD)
    weakening_tiles = jnp.transpose(log_decay.reshape(HEADS_PER_BATCH, count, BLOCK), (1, 0, 2))
    gains = gain.reshape(HEADS_PER_BATCH, HD)

    def step(state, items):
        state, inside = block_step(state, items[0], items[1], items[2], items[3])
        scale = lax.rsqrt(lax.optimization_barrier(jnp.mean(inside * inside, axis=-1, keepdims=True)) + 1e-06)
        return (state, (inside * scale * gains).astype(jnp.bfloat16))
    start = jnp.zeros((HEADS_PER_BATCH, HD, HD), jnp.float32)
    final, outputs = lax.scan(step, start, (q_blocks, k_blocks, v_blocks, weakening_tiles))
    return outputs.reshape(SEQUENCE_SPAN, HEADS_PER_BATCH * HD)
```

```python
import jax
import jax.numpy as jnp
from jax import lax
from jax.experimental import pallas as pl
from jax.experimental.pallas import tpu as pltpu
from jax.sharding import PartitionSpec as P

HEADS = 8
HD = 128
BLOCK = 512
TILE = 128
NY, NX, NZ = 4, 4, 8
HALF = HD // 2
SLAB = HALF + 8
MSG = HD + 8
MESH = pl.DeviceIdType.MESH
F32, BF16 = jnp.float32, jnp.bfloat16
SPLIT = (5, 1, 1, 1)


def order(i):
    return 4 + ((i + 1) // 2) * (1 - 2 * (i % 2))


def kernel(
    q_hbm, k_hbm, v_hbm, ld_hbm, gain_hbm, out_hbm,
    q_s, k_s, v_s, ld_s, gain_s, rows_s, cols_s, e_s, sblk_s, y_s, o_s,
    msg_s, peer_s, zs_s, zr_s, w_s, gp_s, xs_s, xr_s, ys_s, yr_s, cs_s, carry_s,
    q_sem, k_sem, v_sem, o_sem, small_sem,
    core_ss, core_rs, z_ss, z_rs, x_ss, x_rs, y_ss, y_rs, b_ss, b_rs, f_ss, f_rs,
):
    seg, ctx = lax.axis_index("seg"), lax.axis_index("ctx")
    y, x = seg // NX, seg % NX
    z, c = ctx // 2, ctx % 2
    tokens = k_s.shape[1]
    blocks = tokens // BLOCK
    tiles = BLOCK // TILE

    def head_of(i):
        return (z + order(i)) % NZ

    def columns(h):
        return pl.ds(pl.multiple_of(h * HD, HD), HD)

    def at_z(other):
        return (seg, other * 2 + c)

    def at_x(other):
        return (y * NX + other, ctx)

    def at_y(other):
        return (other * NX + x, ctx)

    partner = (seg, z * 2 + (1 - c))

    barrier = pltpu.get_barrier_semaphore()

    def signal(device):
        pl.semaphore_signal(barrier, inc=1, device_id=device, device_id_type=MESH)

    ld_copy = pltpu.make_async_copy(ld_hbm, ld_s, small_sem.at[0])
    gain_copy = pltpu.make_async_copy(gain_hbm, gain_s, small_sem.at[1])
    ld_copy.start()

    def load(hbm, vmem, sem, h):
        return pltpu.make_async_copy(hbm.at[:, columns(h)], vmem.at[h], sem.at[h])

    def start_kv(i, _):
        h = head_of(i)
        load(k_hbm, k_s, k_sem, h).start()
        load(v_hbm, v_s, v_sem, h).start()
        return 0

    lax.fori_loop(0, HEADS, start_kv, 0)
    gain_copy.start()

    def start_q(h, _):
        load(q_hbm, q_s, q_sem, h).start()
        return 0

    lax.fori_loop(0, HEADS, start_q, 0)
    signal(partner)
    for d in range(1, NZ):
        signal(at_z((z + d) % NZ))
    for d in range(1, NX):
        signal(at_x((x + d) % NX))
    for d in range(1, NY):
        signal(at_y((y + d) % NY))

    ld_copy.wait()
    count = tokens // TILE
    stacked = jnp.concatenate([ld_s[:, j * TILE : (j + 1) * TILE] for j in range(count)], axis=0)
    rows = lax.broadcasted_iota(jnp.int32, (TILE, TILE), 0)
    cols = lax.broadcasted_iota(jnp.int32, (TILE, TILE), 1)
    upto = (rows <= cols).astype(F32)
    within = jnp.dot(stacked, upto, precision=lax.Precision.HIGHEST, preferred_element_type=F32)
    within = [within[j * HEADS : (j + 1) * HEADS] for j in range(count)]
    col_c, col_r = [], []
    total = jnp.zeros((HEADS, 1), F32)
    for b in range(blocks):
        start = [jnp.zeros((HEADS, 1), F32)]
        cum = []
        for a in range(tiles):
            w = within[b * tiles + a]
            cum.append(w + start[a])
            start.append(start[a] + w[:, TILE - 1 : TILE])
            col_r.append(jnp.exp(w))
        last = start[tiles]
        col_c += cum
        for a in range(tiles):
            place = slice((b * tiles + a) * TILE, (b * tiles + a + 1) * TILE)
            rows_s[:, 0, place] = cum[a]
            rows_s[:, 4, place] = jnp.exp(last - cum[a])
            for m in range(a + 1, tiles):
                rows_s[:, m, place] = jnp.exp(start[m] - cum[a])
        e_s[:, b, :] = jnp.broadcast_to(jnp.exp(last), (HEADS, HD))
        total = total + last
    e_s[:, blocks, :] = jnp.broadcast_to(jnp.exp(total), (HEADS, HD))
    blank = jnp.zeros((TILE - count * HEADS, TILE), F32)
    cols_s[0] = jnp.transpose(jnp.concatenate(col_c + [blank], axis=0))
    cols_s[1] = jnp.transpose(jnp.concatenate(col_r + [blank], axis=0))
    cols_s[2] = jnp.exp(cols_s[0])

    def to_partner(h):
        return pltpu.make_async_remote_copy(
            src_ref=msg_s.at[h], dst_ref=peer_s.at[h], send_sem=core_ss.at[h], recv_sem=core_rs.at[h],
            device_id=partner, device_id_type=MESH,
        )

    def to_owner(h):
        return pltpu.make_async_remote_copy(
            src_ref=zs_s.at[h], dst_ref=zr_s.at[z], send_sem=z_ss.at[h], recv_sem=z_rs.at[z],
            device_id=at_z(h), device_id_type=MESH,
        )

    def from_shard(other):
        return pltpu.make_async_remote_copy(
            src_ref=zs_s.at[other], dst_ref=zr_s.at[other], send_sem=z_ss.at[other], recv_sem=z_rs.at[other],
            device_id=at_z(other), device_id_type=MESH,
        )

    def own_state(i):
        h = head_of(i)
        load(k_hbm, k_s, k_sem, h).wait()
        load(v_hbm, v_s, v_sem, h).wait()
        state = None
        for b in range(blocks):
            place = slice(b * BLOCK, (b + 1) * BLOCK)
            turned = jnp.transpose(k_s[h, place, :]).astype(F32)
            decayed = (turned * rows_s[h, 4:5, place]).astype(BF16)
            added = jnp.dot(decayed, v_s[h, place, :], preferred_element_type=F32)
            if b:
                sblk_s[h, b - 1] = state
                state = e_s[h, b : b + 1, :] * state + added
            else:
                state = added
        msg_s[h, 0:8, :] = jnp.broadcast_to(e_s[h, blocks : blocks + 1, :], (8, HD))
        msg_s[h, 8:MSG, :] = state

    def pair_state(i):
        h = head_of(i)
        to_partner(h).wait_recv()
        mine, other = msg_s[h, 0:8, :], peer_s[h, 0:8, :]
        half = pl.ds(pl.multiple_of(8 + c * HALF, 8), HALF)
        first = c == 0
        scale_mine = jnp.where(first, other, 1.0)[0:1]
        scale_other = jnp.where(first, 1.0, mine)[0:1]
        joined = scale_mine * msg_s[h, half, :] + scale_other * peer_s[h, half, :]
        zs_s[h, 0:8, :] = mine * other
        zs_s[h, 8:SLAB, :] = joined

        @pl.when(h != z)
        def _():
            to_owner(h).start()

        @pl.when(h == z)
        def _():
            zr_s[z, 0:8, :] = mine * other
            zr_s[z, 8:SLAB, :] = joined

    own_state(0)
    pl.semaphore_wait(barrier, 1 + (NZ - 1) + (NX - 1) + (NY - 1))
    to_partner(head_of(0)).start()
    own_state(1)
    to_partner(head_of(1)).start()

    def states(i, _):
        own_state(i)
        to_partner(head_of(i)).start()
        pair_state(i - 2)
        return 0

    lax.fori_loop(2, HEADS, states, 0)

    below = cols <= rows

    def attend(h, _):
        load(q_hbm, q_s, q_sem, h).wait()
        shift = (HD - h) % HD
        col_c = pltpu.roll(cols_s[0], shift, 1)
        col_r = pltpu.roll(cols_s[1], shift, 1)
        for b in range(blocks):
            for a in range(tiles):
                j = b * tiles + a
                here = slice(j * TILE, (j + 1) * TILE)
                seen = slice(b * BLOCK, (j + 1) * TILE)
                before = slice(b * BLOCK, j * TILE)
                scores = lax.dot_general(
                    q_s[h, here, :], k_s[h, seen, :], (((1,), (1,)), ((), ())), preferred_element_type=F32
                )
                spread = col_c[:, j * HEADS : j * HEADS + 1] - rows_s[h, 0:1, here]
                decay = jnp.where(below, jnp.exp(jnp.minimum(spread, 0.0)), 0.0)
                weights = (scores[:, a * TILE :] * decay).astype(BF16)
                if a:
                    fade = col_r[:, j * HEADS : j * HEADS + 1] * rows_s[h, a : a + 1, before]
                    weights = jnp.concatenate([(scores[:, : a * TILE] * fade).astype(BF16), weights], axis=1)
                y_s[h, here, :] = jnp.dot(weights, v_s[h, seen, :], preferred_element_type=F32)
        return 0

    pair_state(HEADS - 2)
    pair_state(HEADS - 1)
    marks = [0]
    for n in SPLIT:
        marks.append(marks[-1] + n)
    lax.fori_loop(marks[0], marks[1], attend, 0)

    def arrived(i, _):
        from_shard(head_of(i)).wait_recv()
        return 0

    lax.fori_loop(0, NZ - 1, arrived, 0)

    def fold(n, held):
        state, decay = held
        w_s[n] = state
        gp_s[n] = decay
        g = zr_s[n, 0:8, :]
        return (g[0:1] * state + zr_s[n, 8:SLAB, :], decay * g)

    empty = (jnp.zeros((HALF, HD), F32), jnp.ones((8, HD), F32))
    state, decay = lax.fori_loop(0, NZ, fold, empty)

    def exchange(state, decay, buf, got, ss, rs, me, size, at):
        buf[0:8, :] = decay
        buf[8:SLAB, :] = state
        got[me, 0:8, :] = decay
        got[me, 8:SLAB, :] = state

        def copy(d, sending):
            other = (me + d) % size if sending else (me + size - d) % size
            return pltpu.make_async_remote_copy(
                src_ref=buf, dst_ref=got.at[me if sending else other], send_sem=ss.at[d - 1], recv_sem=rs.at[d - 1],
                device_id=at(other), device_id_type=MESH,
            )

        for d in range(1, size):
            copy(d, True).start()
        return copy

    def collect(copy, got, me, size):
        for d in range(1, size):
            copy(d, False).wait_recv()
        state, decay = empty
        before, faded = empty
        for n in range(size):
            mine = me == n
            before, faded = jnp.where(mine, state, before), jnp.where(mine, decay, faded)
            g = got[n, 0:8, :]
            state, decay = g[0:1] * state + got[n, 8:SLAB, :], decay * g
        return before, faded, state, decay

    copy_x = exchange(state, decay, xs_s, xr_s, x_ss, x_rs, x, NX, at_x)
    lax.fori_loop(marks[1], marks[2], attend, 0)
    before_x, faded_x, state, decay = collect(copy_x, xr_s, x, NX)
    copy_y = exchange(state, decay, ys_s, yr_s, y_ss, y_rs, y, NY, at_y)
    lax.fori_loop(marks[2], marks[3], attend, 0)
    before_y, _, _, _ = collect(copy_y, yr_s, y, NY)
    entering = faded_x[0:1] * before_y + before_x

    mine_half = pl.ds(pl.multiple_of(c * HALF, 8), HALF)
    other_half = pl.ds(pl.multiple_of((1 - c) * HALF, 8), HALF)

    def back(other, slot):
        return pltpu.make_async_remote_copy(
            src_ref=cs_s.at[other], dst_ref=carry_s.at[slot, mine_half, :], send_sem=b_ss.at[other], recv_sem=b_rs.at[slot],
            device_id=at_z(other), device_id_type=MESH,
        )

    def give(i, _):
        other = head_of(i)
        value = gp_s[other, 0:1, :] * entering + w_s[other]
        cs_s[other] = value
        back(other, z).start()
        return 0

    def forward(h):
        return pltpu.make_async_remote_copy(
            src_ref=carry_s.at[h, mine_half, :], dst_ref=carry_s.at[h, mine_half, :], send_sem=f_ss.at[h], recv_sem=f_rs.at[h],
            device_id=partner, device_id_type=MESH,
        )

    def forwarded(h):
        return pltpu.make_async_remote_copy(
            src_ref=carry_s.at[h, other_half, :], dst_ref=carry_s.at[h, other_half, :], send_sem=f_ss.at[h], recv_sem=f_rs.at[h],
            device_id=partner, device_id_type=MESH,
        )

    lax.fori_loop(0, NZ - 1, give, 0)
    carry_s[z, mine_half, :] = gp_s[z, 0:1, :] * entering + w_s[z]
    forward(z).start()
    lax.fori_loop(marks[3], marks[4], attend, 0)

    gain_copy.wait()

    def store(h):
        return pltpu.make_async_copy(o_s.at[h], out_hbm.at[:, columns(h)], o_sem.at[h])

    def pass_on(i):
        h = head_of(i)
        back(h, h).wait_recv()
        forward(h).start()

    def finish(i):
        h = head_of(i)
        forwarded(h).wait_recv()
        carry = carry_s[h]
        carry = jnp.where(c == 0, carry, peer_s[h, 0:1, :] * carry + peer_s[h, 8:MSG, :])
        gain = gain_s[h]
        col_e = pltpu.roll(cols_s[2], (HD - h) % HD, 1)
        for b in range(blocks):
            if b:
                carry = e_s[h, b - 1 : b, :] * carry
                start = carry + sblk_s[h, b - 1]
            else:
                start = carry
            high = start.astype(BF16)
            low = (start - high.astype(F32)).astype(BF16)
            both = jnp.concatenate([high, low], axis=0)
            place = slice(b * BLOCK, (b + 1) * BLOCK)
            query = q_s[h, place, :]
            through = jnp.dot(jnp.concatenate([query, query], axis=1), both, preferred_element_type=F32)
            for a in range(tiles):
                j = b * tiles + a
                here = slice(j * TILE, (j + 1) * TILE)
                value = y_s[h, here, :] + col_e[:, j * HEADS : j * HEADS + 1] * through[a * TILE : (a + 1) * TILE]
                scale = lax.rsqrt(jnp.mean(value * value, axis=-1, keepdims=True) + 1e-06)
                o_s[h, here, :] = (value * scale * gain).astype(BF16)
        store(h).start()

    def outputs(n, _):
        pass_on(HEADS - 1 - n - 1)
        finish(HEADS - 1 - n)
        return 0

    lax.fori_loop(0, HEADS - 1, outputs, 0)
    finish(0)

    def drain(h, _):
        to_partner(h).wait_send()
        forward(h).wait_send()
        store(h).wait()

        @pl.when(h != z)
        def _():
            to_owner(h).wait_send()
            back(h, z).wait_send()

        return 0

    lax.fori_loop(0, HEADS, drain, 0)
    for d in range(1, NX):
        copy_x(d, True).wait_send()
    for d in range(1, NY):
        copy_y(d, True).wait_send()


def shards(queries, keys, values, log_decay, gain):
    tokens = queries.shape[0]
    blocks = tokens // BLOCK
    heads = (HEADS, tokens, HD)
    vmem, dma = pltpu.VMEM, pltpu.SemaphoreType.DMA
    scratch = [
        vmem(heads, BF16), vmem(heads, BF16), vmem(heads, BF16),
        vmem((HEADS, tokens), F32), vmem((HEADS, 1, HD), F32),
        vmem((HEADS, 5, tokens), F32), vmem((3, TILE, TILE), F32), vmem((HEADS, blocks + 1, HD), F32),
        vmem((HEADS, blocks - 1, HD, HD), F32), vmem(heads, F32), vmem(heads, BF16),
        vmem((HEADS, MSG, HD), F32), vmem((HEADS, MSG, HD), F32),
        vmem((NZ, SLAB, HD), F32), vmem((NZ, SLAB, HD), F32),
        vmem((NZ, HALF, HD), F32), vmem((NZ, 8, HD), F32),
        vmem((SLAB, HD), F32), vmem((NX, SLAB, HD), F32),
        vmem((SLAB, HD), F32), vmem((NY, SLAB, HD), F32),
        vmem((NZ, HALF, HD), F32), vmem((HEADS, HD, HD), F32),
        dma((HEADS,)), dma((HEADS,)), dma((HEADS,)), dma((HEADS,)), dma((2,)),
        dma((HEADS,)), dma((HEADS,)), dma((NZ,)), dma((NZ,)),
        dma((NX - 1,)), dma((NX - 1,)), dma((NY - 1,)), dma((NY - 1,)),
        dma((NZ,)), dma((NZ,)), dma((HEADS,)), dma((HEADS,)),
    ]
    return pl.pallas_call(
        kernel,
        out_shape=jax.ShapeDtypeStruct(queries.shape, BF16),
        in_specs=[pl.BlockSpec(memory_space=pl.ANY)] * 5,
        out_specs=pl.BlockSpec(memory_space=pl.ANY),
        scratch_shapes=scratch,
        compiler_params=pltpu.CompilerParams(
            collective_id=0, has_side_effects=True, vmem_limit_bytes=48 * 1024 * 1024
        ),
        cost_estimate=pl.CostEstimate(flops=4 * 10**9, bytes_accessed=13 * 10**6, transcendentals=2 * 10**6),
    )(queries, keys, values, log_decay, gain.reshape(HEADS, 1, HD))


def solution(mesh):
    in_specs = (
        P(("seg", "ctx"), None),
        P(("seg", "ctx"), None),
        P(("seg", "ctx"), None),
        P(None, ("seg", "ctx")),
        P(),
    )
    out_specs = P(("seg", "ctx"), None)
    return jax.shard_map(shards, mesh=mesh, in_specs=in_specs, out_specs=out_specs, check_vma=False)
```

```python
import jax
import jax.numpy as jnp
from jax import lax
from jax.experimental import pallas as pl
from jax.experimental.pallas import tpu as pltpu
from jax.sharding import PartitionSpec as P

HEADS = 8
HD = 128
BLOCK = 512
TILE = 128
NSEG, NZ = 16, 8
HALF = HD // 2
EARLY = 4
SLAB = HALF + 8
MSG = HD + 8
LOG2E = 1.4426950408889634
MESH = pl.DeviceIdType.MESH
F32, BF16 = jnp.float32, jnp.bfloat16
SPLIT = (3, 2, 3)


def order(i):
    return 4 + ((i + 1) // 2) * (1 - 2 * (i % 2))


def kernel(
    q_hbm, k_hbm, v_hbm, ld_hbm, gain_hbm, out_hbm,
    q_s, k_s, v_s, ld_s, gain_s, rows_s, cols_s, e_s, sblk_s, y_s, r_s, o_s,
    msg_s, peer_s, zs_s, zr_s, w_s, gp_s, t_s, got_s, cs_s, carry_s,
    q_sem, k_sem, v_sem, o_sem, small_sem,
    core_ss, core_rs, z_ss, z_rs, t_ss, t_rs, b_ss, b_rs, f_ss, f_rs, ready_sem,
):
    seg, ctx = lax.axis_index("seg"), lax.axis_index("ctx")
    z, c = ctx // 2, ctx % 2
    tokens = k_s.shape[1]
    blocks = tokens // BLOCK
    tiles = BLOCK // TILE

    def head_of(i):
        return (z + order(i)) % NZ

    def columns(h):
        return pl.ds(pl.multiple_of(h * HD, HD), HD)

    def at_z(other):
        return (seg, other * 2 + c)

    def at_seg(other):
        return (other, ctx)

    partner = (seg, z * 2 + (1 - c))

    barrier = pltpu.get_barrier_semaphore()

    def signal(device):
        pl.semaphore_signal(barrier, inc=1, device_id=device, device_id_type=MESH)

    for i in range(NZ - 1):
        signal(at_z(head_of(i)))
    signal(partner)
    ld_copy = pltpu.make_async_copy(ld_hbm, ld_s, small_sem.at[0])
    gain_copy = pltpu.make_async_copy(gain_hbm, gain_s, small_sem.at[1])
    ld_copy.start()

    def load(hbm, vmem, sem, h):
        return pltpu.make_async_copy(hbm.at[:, columns(h)], vmem.at[h], sem.at[h])

    def start_kv(i, _):
        h = head_of(i)
        load(k_hbm, k_s, k_sem, h).start()
        load(v_hbm, v_s, v_sem, h).start()
        return 0

    lax.fori_loop(0, HEADS, start_kv, 0)
    gain_copy.start()

    def start_q(h, _):
        load(q_hbm, q_s, q_sem, h).start()
        return 0

    lax.fori_loop(0, HEADS, start_q, 0)

    def greet(other, _):
        signal(at_seg(other))
        return 0

    lax.fori_loop(seg + 1, NSEG, greet, 0)

    ld_copy.wait()
    count = tokens // TILE
    stacked = jnp.concatenate([ld_s[:, j * TILE : (j + 1) * TILE] for j in range(count)], axis=0) * LOG2E
    rows = lax.broadcasted_iota(jnp.int32, (TILE, TILE), 0)
    cols = lax.broadcasted_iota(jnp.int32, (TILE, TILE), 1)
    upto = (rows <= cols).astype(F32)
    within = jnp.dot(stacked, upto, precision=lax.Precision.HIGHEST, preferred_element_type=F32)
    within = [within[j * HEADS : (j + 1) * HEADS] for j in range(count)]
    col_c, col_r = [], []
    total = jnp.zeros((HEADS, 1), F32)
    for b in range(blocks):
        start = [jnp.zeros((HEADS, 1), F32)]
        cum = []
        for a in range(tiles):
            w = within[b * tiles + a]
            cum.append(w + start[a])
            start.append(start[a] + w[:, TILE - 1 : TILE])
            col_r.append(jnp.exp2(w))
        last = start[tiles]
        col_c += cum
        for a in range(tiles):
            place = slice((b * tiles + a) * TILE, (b * tiles + a + 1) * TILE)
            rows_s[:, 0, place] = cum[a]
            rows_s[:, 4, place] = jnp.exp2(last - cum[a])
            for m in range(a + 1, tiles):
                rows_s[:, m, place] = jnp.exp2(start[m] - cum[a])
        e_s[:, b, :] = jnp.broadcast_to(jnp.exp2(last), (HEADS, HD))
        total = total + last
    e_s[:, blocks, :] = jnp.broadcast_to(jnp.exp2(total), (HEADS, HD))
    blank = jnp.zeros((TILE - count * HEADS, TILE), F32)
    cols_s[0] = jnp.transpose(jnp.concatenate(col_c + [blank], axis=0))
    cols_s[1] = jnp.transpose(jnp.concatenate(col_r + [blank], axis=0))

    def to_partner(h):
        return pltpu.make_async_remote_copy(
            src_ref=msg_s.at[h], dst_ref=peer_s.at[h], send_sem=core_ss.at[h], recv_sem=core_rs.at[h],
            device_id=partner, device_id_type=MESH,
        )

    def to_owner(h):
        return pltpu.make_async_remote_copy(
            src_ref=zs_s.at[h], dst_ref=zr_s.at[z], send_sem=z_ss.at[h], recv_sem=z_rs.at[z],
            device_id=at_z(h), device_id_type=MESH,
        )

    def from_shard(other):
        return pltpu.make_async_remote_copy(
            src_ref=zs_s.at[other], dst_ref=zr_s.at[other], send_sem=z_ss.at[other], recv_sem=z_rs.at[other],
            device_id=at_z(other), device_id_type=MESH,
        )

    def own_state(i):
        h = head_of(i)
        load(k_hbm, k_s, k_sem, h).wait()
        load(v_hbm, v_s, v_sem, h).wait()
        state = None
        for b in range(blocks):
            place = slice(b * BLOCK, (b + 1) * BLOCK)
            turned = jnp.transpose(k_s[h, place, :]).astype(F32)
            decayed = (turned * rows_s[h, 4:5, place]).astype(BF16)
            added = jnp.dot(decayed, v_s[h, place, :], preferred_element_type=F32)
            if b:
                sblk_s[h, b - 1] = state
                state = e_s[h, b : b + 1, :] * state + added
            else:
                state = added
        msg_s[h, 0:8, :] = jnp.broadcast_to(e_s[h, blocks : blocks + 1, :], (8, HD))
        msg_s[h, 8:MSG, :] = state

    def pair_state(i):
        h = head_of(i)
        to_partner(h).wait_recv()
        mine, other = msg_s[h, 0:8, :], peer_s[h, 0:8, :]
        half = pl.ds(pl.multiple_of(8 + c * HALF, 8), HALF)
        first = c == 0
        scale_mine = jnp.where(first, other, 1.0)[0:1]
        scale_other = jnp.where(first, 1.0, mine)[0:1]
        joined = scale_mine * msg_s[h, half, :] + scale_other * peer_s[h, half, :]
        zs_s[h, 0:8, :] = mine * other
        zs_s[h, 8:SLAB, :] = joined

        @pl.when(h != z)
        def _():
            to_owner(h).start()

        @pl.when(h == z)
        def _():
            zr_s[z, 0:8, :] = mine * other
            zr_s[z, 8:SLAB, :] = joined

    def states(i, _):
        own_state(i)
        return 0

    def send_states(i, _):
        to_partner(head_of(i)).start()
        return 0

    def joint(i, _):
        pair_state(i - EARLY)
        own_state(i)
        to_partner(head_of(i)).start()
        return 0

    def pair_states(i, _):
        pair_state(i)
        return 0

    def ready(other, _):
        pl.semaphore_signal(ready_sem, inc=1, device_id=at_seg(other), device_id_type=MESH)
        return 0

    lax.fori_loop(0, EARLY, states, 0)
    pl.semaphore_wait(barrier, 1 + (NZ - 1) + seg)
    lax.fori_loop(0, EARLY, send_states, 0)
    lax.fori_loop(EARLY, HEADS, joint, 0)
    lax.fori_loop(HEADS - EARLY, HEADS, pair_states, 0)
    lax.fori_loop(0, seg, ready, 0)

    below = cols <= rows

    def attend(h, _):
        load(q_hbm, q_s, q_sem, h).wait()
        shift = (HD - h) % HD
        col_c = pltpu.roll(cols_s[0], shift, 1)
        col_r = pltpu.roll(cols_s[1], shift, 1)
        for b in range(blocks):
            for a in range(tiles):
                j = b * tiles + a
                here = slice(j * TILE, (j + 1) * TILE)
                query = q_s[h, here, :]
                cum = jnp.broadcast_to(col_c[:, j * HEADS : j * HEADS + 1], (TILE, TILE))
                r_s[h, here, :] = jnp.exp2(cum)
                if a:
                    fade = jnp.broadcast_to(col_r[:, j * HEADS : j * HEADS + 1], (TILE, TILE))
                sums = None
                for first in range(0, a + 1, 2):
                    seen = range(first, min(first + 2, a + 1))
                    piece = slice((b * tiles + first) * TILE, (b * tiles + seen[-1] + 1) * TILE)
                    scores = lax.dot_general(
                        query, k_s[h, piece, :], (((1,), (1,)), ((), ())), preferred_element_type=F32
                    )
                    weights = []
                    for n, m in enumerate(seen):
                        score = scores[:, n * TILE : (n + 1) * TILE]
                        there = slice((b * tiles + m) * TILE, (b * tiles + m + 1) * TILE)
                        if m < a:
                            score = score * rows_s[h, a : a + 1, there] * fade
                        else:
                            score = score * jnp.where(below, jnp.exp2(cum - rows_s[h, 0:1, there]), 0.0)
                        weights.append(score.astype(BF16))
                    if len(weights) > 1:
                        weights = [jnp.concatenate(weights, axis=1)]
                    part = jnp.dot(weights[0], v_s[h, piece, :], preferred_element_type=F32)
                    sums = part if sums is None else sums + part
                y_s[h, here, :] = sums
        return 0

    marks = [0]
    for n in SPLIT:
        marks.append(marks[-1] + n)
    lax.fori_loop(marks[0], marks[1], attend, 0)

    def fold(n, held):
        state, decay = held

        @pl.when(n != z)
        def _():
            from_shard(n).wait_recv()

        w_s[n] = state
        gp_s[n] = decay
        g = zr_s[n, 0:8, :]
        return (g[0:1] * state + zr_s[n, 8:SLAB, :], decay * g)

    empty = (jnp.zeros((HALF, HD), F32), jnp.ones((8, HD), F32))
    state, decay = lax.fori_loop(0, NZ, fold, empty)
    t_s[0:8, :] = decay
    t_s[8:SLAB, :] = state

    def to_seg(other):
        return pltpu.make_async_remote_copy(
            src_ref=t_s, dst_ref=got_s.at[seg], send_sem=t_ss.at[other], recv_sem=t_rs.at[seg],
            device_id=at_seg(other), device_id_type=MESH,
        )

    def from_seg(other):
        return pltpu.make_async_remote_copy(
            src_ref=t_s, dst_ref=got_s.at[other], send_sem=t_ss.at[other], recv_sem=t_rs.at[other],
            device_id=at_seg(other), device_id_type=MESH,
        )

    def tell(n, _):
        to_seg(NSEG - 1 - n).start()
        return 0

    @pl.when(seg < NSEG - 1)
    def _():
        pl.semaphore_wait(ready_sem, NSEG - 1 - seg)

    lax.fori_loop(0, NSEG - 1 - seg, tell, 0)
    lax.fori_loop(marks[1], marks[2], attend, 0)

    def gather(n, entering):
        from_seg(n).wait_recv()
        return got_s[n, 0:1, :] * entering + got_s[n, 8:SLAB, :]

    entering = lax.fori_loop(0, seg, gather, jnp.zeros((HALF, HD), F32))

    mine_half = pl.ds(pl.multiple_of(c * HALF, 8), HALF)
    other_half = pl.ds(pl.multiple_of((1 - c) * HALF, 8), HALF)

    def back(other, slot):
        return pltpu.make_async_remote_copy(
            src_ref=cs_s.at[other], dst_ref=carry_s.at[slot, mine_half, :], send_sem=b_ss.at[other], recv_sem=b_rs.at[slot],
            device_id=at_z(other), device_id_type=MESH,
        )

    def give(n, _):
        other = lax.rem(n + jnp.where(n >= z, 1, 0), NZ)
        value = gp_s[other, 0:1, :] * entering + w_s[other]
        cs_s[other] = value
        back(other, z).start()
        return 0

    def forward(h):
        return pltpu.make_async_remote_copy(
            src_ref=carry_s.at[h, mine_half, :], dst_ref=carry_s.at[h, mine_half, :], send_sem=f_ss.at[h], recv_sem=f_rs.at[h],
            device_id=partner, device_id_type=MESH,
        )

    def forwarded(h):
        return pltpu.make_async_remote_copy(
            src_ref=carry_s.at[h, other_half, :], dst_ref=carry_s.at[h, other_half, :], send_sem=f_ss.at[h], recv_sem=f_rs.at[h],
            device_id=partner, device_id_type=MESH,
        )

    lax.fori_loop(0, NZ - 1, give, 0)
    carry_s[z, mine_half, :] = gp_s[z, 0:1, :] * entering + w_s[z]
    forward(z).start()
    lax.fori_loop(marks[2], marks[3], attend, 0)

    gain_copy.wait()

    def store(h):
        return pltpu.make_async_copy(o_s.at[h], out_hbm.at[:, columns(h)], o_sem.at[h])

    def pass_on(i):
        h = head_of(i)
        back(h, h).wait_recv()
        forward(h).start()

    def finish(i):
        h = head_of(i)
        forwarded(h).wait_recv()
        carry = carry_s[h]
        carry = jnp.where(c == 0, carry, peer_s[h, 0:1, :] * carry + peer_s[h, 8:MSG, :])
        gain = gain_s[h]
        for b in range(blocks):
            if b:
                carry = e_s[h, b - 1 : b, :] * carry
                start = carry + sblk_s[h, b - 1]
            else:
                start = carry
            high = start.astype(BF16)
            low = (start - high.astype(F32)).astype(BF16)
            both = jnp.concatenate([high, low], axis=0)
            for a in range(tiles):
                j = b * tiles + a
                here = slice(j * TILE, (j + 1) * TILE)
                query = q_s[h, here, :]
                through = jnp.dot(jnp.concatenate([query, query], axis=1), both, preferred_element_type=F32)
                value = y_s[h, here, :] + r_s[h, here, :] * through
                scale = lax.rsqrt(jnp.mean(value * value, axis=-1, keepdims=True) + 1e-06)
                o_s[h, here, :] = (value * scale * gain).astype(BF16)
        store(h).start()

    def outputs(n, _):
        pass_on(HEADS - 3 - n)
        finish(HEADS - 1 - n)
        return 0

    pass_on(HEADS - 2)
    lax.fori_loop(0, HEADS - 2, outputs, 0)

    def last_outputs(n, _):
        finish(1 - n)
        return 0

    lax.fori_loop(0, 2, last_outputs, 0)

    def drain(h, _):
        to_partner(h).wait_send()
        forward(h).wait_send()
        store(h).wait()

        @pl.when(h != z)
        def _():
            to_owner(h).wait_send()
            back(h, z).wait_send()

        return 0

    lax.fori_loop(0, HEADS, drain, 0)

    def drain_totals(other, _):
        to_seg(other).wait_send()
        return 0

    lax.fori_loop(seg + 1, NSEG, drain_totals, 0)


def shards(queries, keys, values, log_decay, gain):
    tokens = queries.shape[0]
    blocks = tokens // BLOCK
    heads = (HEADS, tokens, HD)
    vmem, dma = pltpu.VMEM, pltpu.SemaphoreType.DMA
    scratch = [
        vmem(heads, BF16), vmem(heads, BF16), vmem(heads, BF16),
        vmem((HEADS, tokens), F32), vmem((HEADS, 1, HD), F32),
        vmem((HEADS, 5, tokens), F32), vmem((2, TILE, TILE), F32), vmem((HEADS, blocks + 1, HD), F32),
        vmem((HEADS, blocks - 1, HD, HD), F32), vmem(heads, F32), vmem(heads, F32), vmem(heads, BF16),
        vmem((HEADS, MSG, HD), F32), vmem((HEADS, MSG, HD), F32),
        vmem((NZ, SLAB, HD), F32), vmem((NZ, SLAB, HD), F32),
        vmem((NZ, HALF, HD), F32), vmem((NZ, 8, HD), F32),
        vmem((SLAB, HD), F32), vmem((NSEG, SLAB, HD), F32),
        vmem((NZ, HALF, HD), F32), vmem((HEADS, HD, HD), F32),
        dma((HEADS,)), dma((HEADS,)), dma((HEADS,)), dma((HEADS,)), dma((2,)),
        dma((HEADS,)), dma((HEADS,)), dma((NZ,)), dma((NZ,)),
        dma((NSEG,)), dma((NSEG,)), dma((NZ,)), dma((NZ,)), dma((HEADS,)), dma((HEADS,)),
        pltpu.SemaphoreType.REGULAR,
    ]
    operands = (queries, keys, values, log_decay, gain.reshape(HEADS, 1, HD))
    operands = [pltpu.with_memory_space_constraint(a, pltpu.HBM) for a in operands]
    return pl.pallas_call(
        kernel,
        out_shape=jax.ShapeDtypeStruct(queries.shape, BF16),
        in_specs=[pl.BlockSpec(memory_space=pltpu.HBM)] * 5,
        out_specs=pl.BlockSpec(memory_space=pl.ANY),
        scratch_shapes=scratch,
        compiler_params=pltpu.CompilerParams(
            collective_id=0, has_side_effects=True, vmem_limit_bytes=48 * 1024 * 1024
        ),
        cost_estimate=pl.CostEstimate(flops=4 * 10**9, bytes_accessed=13 * 10**6, transcendentals=2 * 10**6),
    )(*operands)


def solution(mesh):
    in_specs = (
        P(("seg", "ctx"), None),
        P(("seg", "ctx"), None),
        P(("seg", "ctx"), None),
        P(None, ("seg", "ctx")),
        P(),
    )
    out_specs = P(("seg", "ctx"), None)
    return jax.shard_map(shards, mesh=mesh, in_specs=in_specs, out_specs=out_specs, check_vma=False)
```

```python
import jax
import jax.numpy as jnp
from jax import lax
from jax.experimental import pallas as pl
from jax.experimental.pallas import tpu as pltpu
from jax.sharding import PartitionSpec as P

HEADS = 8
HD = 128
BLOCK = 512
TILE = 128
NSEG, NZ = 16, 8
HALF = HD // 2
EARLY = 8
SLAB = HALF + 8
MSG = HD + 8
LOG2E = 1.4426950408889634
MESH = pl.DeviceIdType.MESH
F32, BF16 = jnp.float32, jnp.bfloat16
SPLIT = (3, 3, 2)


def order(i):
    return 4 + ((i + 1) // 2) * (1 - 2 * (i % 2))


def kernel(
    q_hbm, k_hbm, v_hbm, ld_hbm, gain_hbm, out_hbm,
    q_s, k_s, v_s, ld_s, gain_s, rows_s, cols_s, e_s, sblk_s, y_s, r_s, o_s,
    msg_s, peer_s, zs_s, zr_s, w_s, gp_s, t_s, got_s, cs_s, carry_s,
    q_sem, k_sem, v_sem, o_sem, small_sem,
    core_ss, core_rs, z_ss, z_rs, t_ss, t_rs, b_ss, b_rs, f_ss, f_rs, ready_sem,
):
    seg, ctx = lax.axis_index("seg"), lax.axis_index("ctx")
    z, c = ctx // 2, ctx % 2
    tokens = k_s.shape[1]
    blocks = tokens // BLOCK
    tiles = BLOCK // TILE

    def head_of(i):
        return (z + order(i)) % NZ

    def columns(h):
        return pl.ds(pl.multiple_of(h * HD, HD), HD)

    def at_z(other):
        return (seg, other * 2 + c)

    def at_seg(other):
        return (other, ctx)

    partner = (seg, z * 2 + (1 - c))

    barrier = pltpu.get_barrier_semaphore()

    def signal(device):
        pl.semaphore_signal(barrier, inc=1, device_id=device, device_id_type=MESH)

    ld_copy = pltpu.make_async_copy(ld_hbm, ld_s, small_sem.at[0])
    gain_copy = pltpu.make_async_copy(gain_hbm, gain_s, small_sem.at[1])
    ld_copy.start()
    gain_copy.start()

    def load(hbm, vmem, sem, h):
        return pltpu.make_async_copy(hbm.at[:, columns(h)], vmem.at[h], sem.at[h])

    def start_kv(i, _):
        h = head_of(i)
        load(k_hbm, k_s, k_sem, h).start()
        load(v_hbm, v_s, v_sem, h).start()
        return 0

    lax.fori_loop(0, HEADS, start_kv, 0)

    def start_q(h, _):
        load(q_hbm, q_s, q_sem, h).start()
        return 0

    def greet_z(other, _):
        signal(at_z(other))
        return 0

    def greet_seg(other, _):
        signal(at_seg(other))
        return 0

    def ready_z(other, _):
        pl.semaphore_signal(ready_sem.at[0], inc=1, device_id=at_z(other), device_id_type=MESH)
        return 0

    def ready_seg(other, _):
        pl.semaphore_signal(ready_sem.at[1], inc=1, device_id=at_seg(other), device_id_type=MESH)
        return 0

    signal(partner)
    lax.fori_loop(z + 1, NZ, greet_z, 0)
    lax.fori_loop(seg + 1, NSEG, greet_seg, 0)
    pl.semaphore_wait(barrier, 1 + z + seg)
    lax.fori_loop(0, z, ready_z, 0)

    ld_copy.wait()
    count = tokens // TILE
    stacked = jnp.concatenate([ld_s[:, j * TILE : (j + 1) * TILE] for j in range(count)], axis=0) * LOG2E
    rows = lax.broadcasted_iota(jnp.int32, (TILE, TILE), 0)
    cols = lax.broadcasted_iota(jnp.int32, (TILE, TILE), 1)
    upto = (rows <= cols).astype(F32)
    within = jnp.dot(stacked, upto, precision=lax.Precision.HIGHEST, preferred_element_type=F32)
    within = [within[j * HEADS : (j + 1) * HEADS] for j in range(count)]
    col_c, col_r = [], []
    total = jnp.zeros((HEADS, 1), F32)
    for b in range(blocks):
        start = [jnp.zeros((HEADS, 1), F32)]
        cum = []
        for a in range(tiles):
            w = within[b * tiles + a]
            cum.append(w + start[a])
            start.append(start[a] + w[:, TILE - 1 : TILE])
            col_r.append(jnp.exp2(w))
        last = start[tiles]
        col_c += cum
        for a in range(tiles):
            place = slice((b * tiles + a) * TILE, (b * tiles + a + 1) * TILE)
            rows_s[:, 0, place] = cum[a]
            rows_s[:, 4, place] = jnp.exp2(last - cum[a])
            for m in range(a + 1, tiles):
                rows_s[:, m, place] = jnp.exp2(start[m] - cum[a])
        e_s[:, b, :] = jnp.broadcast_to(jnp.exp2(last), (HEADS, HD))
        total = total + last
    e_s[:, blocks, :] = jnp.broadcast_to(jnp.exp2(total), (HEADS, HD))
    blank = jnp.zeros((TILE - count * HEADS, TILE), F32)
    cols_s[0] = jnp.transpose(jnp.concatenate(col_c + [blank], axis=0))
    cols_s[1] = jnp.transpose(jnp.concatenate(col_r + [blank], axis=0))

    def to_partner(h):
        return pltpu.make_async_remote_copy(
            src_ref=msg_s.at[h], dst_ref=peer_s.at[h], send_sem=core_ss.at[h], recv_sem=core_rs.at[h],
            device_id=partner, device_id_type=MESH,
        )

    def to_owner(h):
        return pltpu.make_async_remote_copy(
            src_ref=zs_s.at[h], dst_ref=zr_s.at[z], send_sem=z_ss.at[h], recv_sem=z_rs.at[z],
            device_id=at_z(h), device_id_type=MESH,
        )

    def from_shard(other):
        return pltpu.make_async_remote_copy(
            src_ref=zs_s.at[other], dst_ref=zr_s.at[other], send_sem=z_ss.at[other], recv_sem=z_rs.at[other],
            device_id=at_z(other), device_id_type=MESH,
        )

    def own_state(i):
        h = head_of(i)
        load(k_hbm, k_s, k_sem, h).wait()
        load(v_hbm, v_s, v_sem, h).wait()
        state = None
        for b in range(blocks):
            place = slice(b * BLOCK, (b + 1) * BLOCK)
            turned = jnp.transpose(k_s[h, place, :]).astype(F32)
            decayed = (turned * rows_s[h, 4:5, place]).astype(BF16)
            added = jnp.dot(decayed, v_s[h, place, :], preferred_element_type=F32)
            if b:
                sblk_s[h, b - 1] = state
                state = e_s[h, b : b + 1, :] * state + added
            else:
                state = added
        msg_s[h, 0:8, :] = jnp.broadcast_to(e_s[h, blocks : blocks + 1, :], (8, HD))
        msg_s[h, 8:MSG, :] = state

    def pair_state(i):
        h = head_of(i)
        to_partner(h).wait_recv()
        mine, other = msg_s[h, 0:8, :], peer_s[h, 0:8, :]
        half = pl.ds(pl.multiple_of(8 + c * HALF, 8), HALF)
        first = c == 0
        scale_mine = jnp.where(first, other, 1.0)[0:1]
        scale_other = jnp.where(first, 1.0, mine)[0:1]
        joined = scale_mine * msg_s[h, half, :] + scale_other * peer_s[h, half, :]
        zs_s[h, 0:8, :] = mine * other
        zs_s[h, 8:SLAB, :] = joined

        @pl.when(h != z)
        def _():
            to_owner(h).start()

        @pl.when(h == z)
        def _():
            zr_s[z, 0:8, :] = mine * other
            zr_s[z, 8:SLAB, :] = joined

    def states(i, _):
        own_state(i)
        to_partner(head_of(i)).start()
        return 0

    def joint(i, _):
        pair_state(i - EARLY)
        own_state(i)
        to_partner(head_of(i)).start()
        return 0

    def pair_states(i, _):
        pair_state(i)
        return 0

    lax.fori_loop(0, EARLY, states, 0)

    @pl.when(z < NZ - 1)
    def _():
        pl.semaphore_wait(ready_sem.at[0], NZ - 1 - z)

    lax.fori_loop(EARLY, HEADS, joint, 0)
    lax.fori_loop(0, HEADS, start_q, 0)
    lax.fori_loop(HEADS - EARLY, HEADS, pair_states, 0)
    lax.fori_loop(0, seg, ready_seg, 0)

    below = cols <= rows

    def attend(h, _):
        load(q_hbm, q_s, q_sem, h).wait()
        shift = (HD - h) % HD
        col_c = pltpu.roll(cols_s[0], shift, 1)
        col_r = pltpu.roll(cols_s[1], shift, 1)
        for b in range(blocks):
            for a in range(tiles):
                j = b * tiles + a
                here = slice(j * TILE, (j + 1) * TILE)
                query = q_s[h, here, :]
                cum = jnp.broadcast_to(col_c[:, j * HEADS : j * HEADS + 1], (TILE, TILE))
                r_s[h, here, :] = jnp.exp2(cum)
                if a:
                    fade = jnp.broadcast_to(col_r[:, j * HEADS : j * HEADS + 1], (TILE, TILE))
                sums = None
                for first in range(0, a + 1, 2):
                    seen = range(first, min(first + 2, a + 1))
                    piece = slice((b * tiles + first) * TILE, (b * tiles + seen[-1] + 1) * TILE)
                    scores = lax.dot_general(
                        query, k_s[h, piece, :], (((1,), (1,)), ((), ())), preferred_element_type=F32
                    )
                    weights = []
                    for n, m in enumerate(seen):
                        score = scores[:, n * TILE : (n + 1) * TILE]
                        there = slice((b * tiles + m) * TILE, (b * tiles + m + 1) * TILE)
                        if m < a:
                            score = score * rows_s[h, a : a + 1, there] * fade
                        else:
                            score = score * jnp.where(below, jnp.exp2(cum - rows_s[h, 0:1, there]), 0.0)
                        weights.append(score.astype(BF16))
                    if len(weights) > 1:
                        weights = [jnp.concatenate(weights, axis=1)]
                    part = jnp.dot(weights[0], v_s[h, piece, :], preferred_element_type=F32)
                    sums = part if sums is None else sums + part
                y_s[h, here, :] = sums
        return 0

    marks = [0]
    for n in SPLIT:
        marks.append(marks[-1] + n)
    lax.fori_loop(marks[0], marks[1], attend, 0)

    def fold(n, held):
        state, decay = held

        @pl.when(n != z)
        def _():
            from_shard(n).wait_recv()

        w_s[n] = state
        gp_s[n] = decay
        g = zr_s[n, 0:8, :]
        return (g[0:1] * state + zr_s[n, 8:SLAB, :], decay * g)

    empty = (jnp.zeros((HALF, HD), F32), jnp.ones((8, HD), F32))
    state, decay = lax.fori_loop(0, NZ, fold, empty)
    t_s[0:8, :] = decay
    t_s[8:SLAB, :] = state

    def to_seg(other):
        return pltpu.make_async_remote_copy(
            src_ref=t_s, dst_ref=got_s.at[seg], send_sem=t_ss.at[other], recv_sem=t_rs.at[seg],
            device_id=at_seg(other), device_id_type=MESH,
        )

    def from_seg(other):
        return pltpu.make_async_remote_copy(
            src_ref=t_s, dst_ref=got_s.at[other], send_sem=t_ss.at[other], recv_sem=t_rs.at[other],
            device_id=at_seg(other), device_id_type=MESH,
        )

    def tell(n, _):
        to_seg(NSEG - 1 - n).start()
        return 0

    @pl.when(seg < NSEG - 1)
    def _():
        pl.semaphore_wait(ready_sem.at[1], NSEG - 1 - seg)

    lax.fori_loop(0, NSEG - 1 - seg, tell, 0)
    lax.fori_loop(marks[1], marks[2], attend, 0)

    def gather(n, entering):
        from_seg(n).wait_recv()
        return got_s[n, 0:1, :] * entering + got_s[n, 8:SLAB, :]

    entering = lax.fori_loop(0, seg, gather, jnp.zeros((HALF, HD), F32))

    mine_half = pl.ds(pl.multiple_of(c * HALF, 8), HALF)
    other_half = pl.ds(pl.multiple_of((1 - c) * HALF, 8), HALF)

    def back(other, slot):
        return pltpu.make_async_remote_copy(
            src_ref=cs_s.at[other], dst_ref=carry_s.at[slot, mine_half, :], send_sem=b_ss.at[other], recv_sem=b_rs.at[slot],
            device_id=at_z(other), device_id_type=MESH,
        )

    def give(n, _):
        other = lax.rem(n + jnp.where(n >= z, 1, 0), NZ)
        value = gp_s[other, 0:1, :] * entering + w_s[other]
        cs_s[other] = value
        back(other, z).start()
        return 0

    def forward(h):
        return pltpu.make_async_remote_copy(
            src_ref=carry_s.at[h, mine_half, :], dst_ref=carry_s.at[h, mine_half, :], send_sem=f_ss.at[h], recv_sem=f_rs.at[h],
            device_id=partner, device_id_type=MESH,
        )

    def forwarded(h):
        return pltpu.make_async_remote_copy(
            src_ref=carry_s.at[h, other_half, :], dst_ref=carry_s.at[h, other_half, :], send_sem=f_ss.at[h], recv_sem=f_rs.at[h],
            device_id=partner, device_id_type=MESH,
        )

    lax.fori_loop(0, NZ - 1, give, 0)
    carry_s[z, mine_half, :] = gp_s[z, 0:1, :] * entering + w_s[z]
    forward(z).start()
    lax.fori_loop(marks[2], marks[3], attend, 0)

    gain_copy.wait()

    def store(h):
        return pltpu.make_async_copy(o_s.at[h], out_hbm.at[:, columns(h)], o_sem.at[h])

    def pass_on(i):
        h = head_of(i)
        back(h, h).wait_recv()
        forward(h).start()

    def finish(i):
        h = head_of(i)
        forwarded(h).wait_recv()
        carry = carry_s[h]
        carry = jnp.where(c == 0, carry, peer_s[h, 0:1, :] * carry + peer_s[h, 8:MSG, :])
        gain = gain_s[h]
        for b in range(blocks):
            if b:
                carry = e_s[h, b - 1 : b, :] * carry
                start = carry + sblk_s[h, b - 1]
            else:
                start = carry
            high = start.astype(BF16)
            low = (start - high.astype(F32)).astype(BF16)
            both = jnp.concatenate([high, low], axis=0)
            for a in range(tiles):
                j = b * tiles + a
                here = slice(j * TILE, (j + 1) * TILE)
                query = q_s[h, here, :]
                through = jnp.dot(jnp.concatenate([query, query], axis=1), both, preferred_element_type=F32)
                value = y_s[h, here, :] + r_s[h, here, :] * through
                scale = lax.rsqrt(jnp.mean(value * value, axis=-1, keepdims=True) + 1e-06)
                o_s[h, here, :] = (value * scale * gain).astype(BF16)
        store(h).start()

    def outputs(n, _):
        pass_on(HEADS - 3 - n)
        finish(HEADS - 1 - n)
        return 0

    pass_on(HEADS - 2)
    lax.fori_loop(0, HEADS - 2, outputs, 0)

    def last_outputs(n, _):
        finish(1 - n)
        return 0

    lax.fori_loop(0, 2, last_outputs, 0)

    def drain(h, _):
        to_partner(h).wait_send()
        forward(h).wait_send()
        store(h).wait()

        @pl.when(h != z)
        def _():
            to_owner(h).wait_send()
            back(h, z).wait_send()

        return 0

    lax.fori_loop(0, HEADS, drain, 0)

    def drain_totals(other, _):
        to_seg(other).wait_send()
        return 0

    lax.fori_loop(seg + 1, NSEG, drain_totals, 0)


def shards(queries, keys, values, log_decay, gain):
    tokens = queries.shape[0]
    blocks = tokens // BLOCK
    heads = (HEADS, tokens, HD)
    vmem, dma = pltpu.VMEM, pltpu.SemaphoreType.DMA
    scratch = [
        vmem(heads, BF16), vmem(heads, BF16), vmem(heads, BF16),
        vmem((HEADS, tokens), F32), vmem((HEADS, 1, HD), F32),
        vmem((HEADS, 5, tokens), F32), vmem((2, TILE, TILE), F32), vmem((HEADS, blocks + 1, HD), F32),
        vmem((HEADS, blocks - 1, HD, HD), F32), vmem(heads, F32), vmem(heads, F32), vmem(heads, BF16),
        vmem((HEADS, MSG, HD), F32), vmem((HEADS, MSG, HD), F32),
        vmem((NZ, SLAB, HD), F32), vmem((NZ, SLAB, HD), F32),
        vmem((NZ, HALF, HD), F32), vmem((NZ, 8, HD), F32),
        vmem((SLAB, HD), F32), vmem((NSEG, SLAB, HD), F32),
        vmem((NZ, HALF, HD), F32), vmem((HEADS, HD, HD), F32),
        dma((HEADS,)), dma((HEADS,)), dma((HEADS,)), dma((HEADS,)), dma((2,)),
        dma((HEADS,)), dma((HEADS,)), dma((NZ,)), dma((NZ,)),
        dma((NSEG,)), dma((NSEG,)), dma((NZ,)), dma((NZ,)), dma((HEADS,)), dma((HEADS,)),
        pltpu.SemaphoreType.REGULAR((2,)),
    ]
    operands = (queries, keys, values, log_decay, gain.reshape(HEADS, 1, HD))
    operands = [pltpu.with_memory_space_constraint(a, pltpu.HBM) for a in operands]
    return pl.pallas_call(
        kernel,
        out_shape=jax.ShapeDtypeStruct(queries.shape, BF16),
        in_specs=[pl.BlockSpec(memory_space=pltpu.HBM)] * 5,
        out_specs=pl.BlockSpec(memory_space=pl.ANY),
        scratch_shapes=scratch,
        compiler_params=pltpu.CompilerParams(
            collective_id=0, has_side_effects=True, vmem_limit_bytes=48 * 1024 * 1024
        ),
        cost_estimate=pl.CostEstimate(flops=4 * 10**9, bytes_accessed=13 * 10**6, transcendentals=2 * 10**6),
    )(*operands)


def solution(mesh):
    in_specs = (
        P(("seg", "ctx"), None),
        P(("seg", "ctx"), None),
        P(("seg", "ctx"), None),
        P(None, ("seg", "ctx")),
        P(),
    )
    out_specs = P(("seg", "ctx"), None)
    return jax.shard_map(shards, mesh=mesh, in_specs=in_specs, out_specs=out_specs, check_vma=False)
```

```python
import jax
import jax.numpy as jnp
from jax import lax
from jax.experimental import pallas as pl
from jax.experimental.pallas import tpu as pltpu
from jax.sharding import PartitionSpec as P

HEADS = 8
HD = 128
BLOCK = 512
TILE = 128
NSEG, NZ = 16, 8
HALF = HD // 2
EARLY = 8
SLAB = HALF + 8
MSG = HD + 8
LOG2E = 1.4426950408889634
MESH = pl.DeviceIdType.MESH
F32, BF16 = jnp.float32, jnp.bfloat16
SPLIT = (3, 3, 2)


def order(i):
    return 4 + ((i + 1) // 2) * (1 - 2 * (i % 2))


def kernel(
    q_hbm, k_hbm, v_hbm, ld_hbm, gain_hbm, out,
    q_s, k_s, v_s, ld_s, gain_s, rows_s, cols_s, e_s, sblk_s, y_s, r_s,
    msg_s, peer_s, zs_s, zr_s, w_s, gp_s, t_s, got_s, cs_s, carry_s,
    q_sem, k_sem, v_sem, small_sem,
    core_ss, core_rs, z_ss, z_rs, t_ss, t_rs, b_ss, b_rs, f_ss, f_rs, ready_sem,
):
    seg, ctx = lax.axis_index("seg"), lax.axis_index("ctx")
    z, c = ctx // 2, ctx % 2
    tokens = k_s.shape[1]
    blocks = tokens // BLOCK
    tiles = BLOCK // TILE

    def head_of(i):
        return (z + order(i)) % NZ

    def columns(h):
        return pl.ds(pl.multiple_of(h * HD, HD), HD)

    def at_z(other):
        return (seg, other * 2 + c)

    def at_seg(other):
        return (other, ctx)

    partner = (seg, z * 2 + (1 - c))

    barrier = pltpu.get_barrier_semaphore()

    def signal(device):
        pl.semaphore_signal(barrier, inc=1, device_id=device, device_id_type=MESH)

    ld_copy = pltpu.make_async_copy(ld_hbm, ld_s, small_sem.at[0])
    gain_copy = pltpu.make_async_copy(gain_hbm, gain_s, small_sem.at[1])
    ld_copy.start()
    gain_copy.start()

    def load(hbm, vmem, sem, h):
        return pltpu.make_async_copy(hbm.at[:, columns(h)], vmem.at[h], sem.at[h])

    def start_kv(i, _):
        h = head_of(i)
        load(k_hbm, k_s, k_sem, h).start()
        load(v_hbm, v_s, v_sem, h).start()
        return 0

    lax.fori_loop(0, HEADS, start_kv, 0)

    def start_q(h, _):
        load(q_hbm, q_s, q_sem, h).start()
        return 0

    def greet_z(other, _):
        signal(at_z(other))
        return 0

    def greet_seg(other, _):
        signal(at_seg(other))
        return 0

    def ready_z(other, _):
        pl.semaphore_signal(ready_sem.at[0], inc=1, device_id=at_z(other), device_id_type=MESH)
        return 0

    def ready_seg(other, _):
        pl.semaphore_signal(ready_sem.at[1], inc=1, device_id=at_seg(other), device_id_type=MESH)
        return 0

    signal(partner)
    lax.fori_loop(z + 1, NZ, greet_z, 0)
    lax.fori_loop(seg + 1, NSEG, greet_seg, 0)
    pl.semaphore_wait(barrier, 1 + z + seg)
    lax.fori_loop(0, z, ready_z, 0)

    ld_copy.wait()
    count = tokens // TILE
    stacked = jnp.concatenate([ld_s[:, j * TILE : (j + 1) * TILE] for j in range(count)], axis=0) * LOG2E
    rows = lax.broadcasted_iota(jnp.int32, (TILE, TILE), 0)
    cols = lax.broadcasted_iota(jnp.int32, (TILE, TILE), 1)
    upto = (rows <= cols).astype(F32)
    within = jnp.dot(stacked, upto, precision=lax.Precision.HIGHEST, preferred_element_type=F32)
    within = [within[j * HEADS : (j + 1) * HEADS] for j in range(count)]
    col_c, col_r = [], []
    total = jnp.zeros((HEADS, 1), F32)
    for b in range(blocks):
        start = [jnp.zeros((HEADS, 1), F32)]
        cum = []
        for a in range(tiles):
            w = within[b * tiles + a]
            cum.append(w + start[a])
            start.append(start[a] + w[:, TILE - 1 : TILE])
            col_r.append(jnp.exp2(w))
        last = start[tiles]
        col_c += cum
        for a in range(tiles):
            place = slice((b * tiles + a) * TILE, (b * tiles + a + 1) * TILE)
            rows_s[:, 0, place] = cum[a]
            rows_s[:, 4, place] = jnp.exp2(last - cum[a])
            for m in range(a + 1, tiles):
                rows_s[:, m, place] = jnp.exp2(start[m] - cum[a])
        e_s[:, b, :] = jnp.broadcast_to(jnp.exp2(last), (HEADS, HD))
        total = total + last
    e_s[:, blocks, :] = jnp.broadcast_to(jnp.exp2(total), (HEADS, HD))
    blank = jnp.zeros((TILE - count * HEADS, TILE), F32)
    cols_s[0] = jnp.transpose(jnp.concatenate(col_c + [blank], axis=0))
    cols_s[1] = jnp.transpose(jnp.concatenate(col_r + [blank], axis=0))

    def to_partner(h):
        return pltpu.make_async_remote_copy(
            src_ref=msg_s.at[h], dst_ref=peer_s.at[h], send_sem=core_ss.at[h], recv_sem=core_rs.at[h],
            device_id=partner, device_id_type=MESH,
        )

    def to_owner(h):
        return pltpu.make_async_remote_copy(
            src_ref=zs_s.at[h], dst_ref=zr_s.at[z], send_sem=z_ss.at[h], recv_sem=z_rs.at[z],
            device_id=at_z(h), device_id_type=MESH,
        )

    def from_shard(other):
        return pltpu.make_async_remote_copy(
            src_ref=zs_s.at[other], dst_ref=zr_s.at[other], send_sem=z_ss.at[other], recv_sem=z_rs.at[other],
            device_id=at_z(other), device_id_type=MESH,
        )

    def own_state(i):
        h = head_of(i)
        load(k_hbm, k_s, k_sem, h).wait()
        load(v_hbm, v_s, v_sem, h).wait()
        state = None
        for b in range(blocks):
            place = slice(b * BLOCK, (b + 1) * BLOCK)
            turned = jnp.transpose(k_s[h, place, :]).astype(F32)
            decayed = (turned * rows_s[h, 4:5, place]).astype(BF16)
            added = jnp.dot(decayed, v_s[h, place, :], preferred_element_type=F32)
            if b:
                sblk_s[h, b - 1] = state
                state = e_s[h, b : b + 1, :] * state + added
            else:
                state = added
        msg_s[h, 0:8, :] = jnp.broadcast_to(e_s[h, blocks : blocks + 1, :], (8, HD))
        msg_s[h, 8:MSG, :] = state

    def pair_state(i):
        h = head_of(i)
        to_partner(h).wait_recv()
        mine, other = msg_s[h, 0:8, :], peer_s[h, 0:8, :]
        half = pl.ds(pl.multiple_of(8 + c * HALF, 8), HALF)
        first = c == 0
        scale_mine = jnp.where(first, other, 1.0)[0:1]
        scale_other = jnp.where(first, 1.0, mine)[0:1]
        joined = scale_mine * msg_s[h, half, :] + scale_other * peer_s[h, half, :]
        zs_s[h, 0:8, :] = mine * other
        zs_s[h, 8:SLAB, :] = joined

        @pl.when(h != z)
        def _():
            to_owner(h).start()

        @pl.when(h == z)
        def _():
            zr_s[z, 0:8, :] = mine * other
            zr_s[z, 8:SLAB, :] = joined

    def states(i, _):
        own_state(i)
        to_partner(head_of(i)).start()
        return 0

    def joint(i, _):
        pair_state(i - EARLY)
        own_state(i)
        to_partner(head_of(i)).start()
        return 0

    def pair_states(i, _):
        pair_state(i)
        return 0

    lax.fori_loop(0, EARLY, states, 0)

    @pl.when(z < NZ - 1)
    def _():
        pl.semaphore_wait(ready_sem.at[0], NZ - 1 - z)

    lax.fori_loop(EARLY, HEADS, joint, 0)
    lax.fori_loop(0, HEADS, start_q, 0)
    lax.fori_loop(HEADS - EARLY, HEADS, pair_states, 0)
    lax.fori_loop(0, seg, ready_seg, 0)

    below = cols <= rows

    def attend(h, _):
        load(q_hbm, q_s, q_sem, h).wait()
        shift = (HD - h) % HD
        col_c = pltpu.roll(cols_s[0], shift, 1)
        col_r = pltpu.roll(cols_s[1], shift, 1)
        for b in range(blocks):
            for a in range(tiles):
                j = b * tiles + a
                here = slice(j * TILE, (j + 1) * TILE)
                query = q_s[h, here, :]
                cum = jnp.broadcast_to(col_c[:, j * HEADS : j * HEADS + 1], (TILE, TILE))
                r_s[h, here, :] = jnp.exp2(cum)
                if a:
                    fade = jnp.broadcast_to(col_r[:, j * HEADS : j * HEADS + 1], (TILE, TILE))
                sums = None
                for first in range(0, a + 1, 2):
                    seen = range(first, min(first + 2, a + 1))
                    piece = slice((b * tiles + first) * TILE, (b * tiles + seen[-1] + 1) * TILE)
                    scores = lax.dot_general(
                        query, k_s[h, piece, :], (((1,), (1,)), ((), ())), preferred_element_type=F32
                    )
                    weights = []
                    for n, m in enumerate(seen):
                        score = scores[:, n * TILE : (n + 1) * TILE]
                        there = slice((b * tiles + m) * TILE, (b * tiles + m + 1) * TILE)
                        if m < a:
                            score = score * rows_s[h, a : a + 1, there] * fade
                        else:
                            score = score * jnp.where(below, jnp.exp2(cum - rows_s[h, 0:1, there]), 0.0)
                        weights.append(score.astype(BF16))
                    if len(weights) > 1:
                        weights = [jnp.concatenate(weights, axis=1)]
                    part = jnp.dot(weights[0], v_s[h, piece, :], preferred_element_type=F32)
                    sums = part if sums is None else sums + part
                y_s[h, here, :] = sums
        return 0

    marks = [0]
    for n in SPLIT:
        marks.append(marks[-1] + n)
    lax.fori_loop(marks[0], marks[1], attend, 0)

    def fold(n, held):
        state, decay = held

        @pl.when(n != z)
        def _():
            from_shard(n).wait_recv()

        w_s[n] = state
        gp_s[n] = decay
        g = zr_s[n, 0:8, :]
        return (g[0:1] * state + zr_s[n, 8:SLAB, :], decay * g)

    empty = (jnp.zeros((HALF, HD), F32), jnp.ones((8, HD), F32))
    state, decay = lax.fori_loop(0, NZ, fold, empty)
    t_s[0:8, :] = decay
    t_s[8:SLAB, :] = state

    def to_seg(other):
        return pltpu.make_async_remote_copy(
            src_ref=t_s, dst_ref=got_s.at[seg], send_sem=t_ss.at[other], recv_sem=t_rs.at[seg],
            device_id=at_seg(other), device_id_type=MESH,
        )

    def from_seg(other):
        return pltpu.make_async_remote_copy(
            src_ref=t_s, dst_ref=got_s.at[other], send_sem=t_ss.at[other], recv_sem=t_rs.at[other],
            device_id=at_seg(other), device_id_type=MESH,
        )

    def tell(n, _):
        to_seg(NSEG - 1 - n).start()
        return 0

    @pl.when(seg < NSEG - 1)
    def _():
        pl.semaphore_wait(ready_sem.at[1], NSEG - 1 - seg)

    lax.fori_loop(0, NSEG - 1 - seg, tell, 0)
    lax.fori_loop(marks[1], marks[2], attend, 0)

    def gather(n, entering):
        from_seg(n).wait_recv()
        return got_s[n, 0:1, :] * entering + got_s[n, 8:SLAB, :]

    entering = lax.fori_loop(0, seg, gather, jnp.zeros((HALF, HD), F32))

    mine_half = pl.ds(pl.multiple_of(c * HALF, 8), HALF)
    other_half = pl.ds(pl.multiple_of((1 - c) * HALF, 8), HALF)

    def back(other, slot):
        return pltpu.make_async_remote_copy(
            src_ref=cs_s.at[other], dst_ref=carry_s.at[slot, mine_half, :], send_sem=b_ss.at[other], recv_sem=b_rs.at[slot],
            device_id=at_z(other), device_id_type=MESH,
        )

    def give(n, _):
        other = lax.rem(n + jnp.where(n >= z, 1, 0), NZ)
        value = gp_s[other, 0:1, :] * entering + w_s[other]
        cs_s[other] = value
        back(other, z).start()
        return 0

    def forward(h):
        return pltpu.make_async_remote_copy(
            src_ref=carry_s.at[h, mine_half, :], dst_ref=carry_s.at[h, mine_half, :], send_sem=f_ss.at[h], recv_sem=f_rs.at[h],
            device_id=partner, device_id_type=MESH,
        )

    def forwarded(h):
        return pltpu.make_async_remote_copy(
            src_ref=carry_s.at[h, other_half, :], dst_ref=carry_s.at[h, other_half, :], send_sem=f_ss.at[h], recv_sem=f_rs.at[h],
            device_id=partner, device_id_type=MESH,
        )

    lax.fori_loop(0, NZ - 1, give, 0)
    carry_s[z, mine_half, :] = gp_s[z, 0:1, :] * entering + w_s[z]
    forward(z).start()
    lax.fori_loop(marks[2], marks[3], attend, 0)

    gain_copy.wait()

    def pass_on(i):
        h = head_of(i)
        back(h, h).wait_recv()
        forward(h).start()

    def finish(i):
        h = head_of(i)
        forwarded(h).wait_recv()
        carry = carry_s[h]
        carry = jnp.where(c == 0, carry, peer_s[h, 0:1, :] * carry + peer_s[h, 8:MSG, :])
        gain = gain_s[h]
        for b in range(blocks):
            if b:
                carry = e_s[h, b - 1 : b, :] * carry
                start = carry + sblk_s[h, b - 1]
            else:
                start = carry
            high = start.astype(BF16)
            low = (start - high.astype(F32)).astype(BF16)
            both = jnp.concatenate([high, low], axis=0)
            for a in range(tiles):
                j = b * tiles + a
                here = slice(j * TILE, (j + 1) * TILE)
                query = q_s[h, here, :]
                through = jnp.dot(jnp.concatenate([query, query], axis=1), both, preferred_element_type=F32)
                value = y_s[h, here, :] + r_s[h, here, :] * through
                scale = lax.rsqrt(jnp.mean(value * value, axis=-1, keepdims=True) + 1e-06)
                out[here, columns(h)] = (value * scale * gain).astype(BF16)

    def outputs(n, _):
        pass_on(HEADS - 3 - n)
        finish(HEADS - 1 - n)
        return 0

    pass_on(HEADS - 2)
    lax.fori_loop(0, HEADS - 2, outputs, 0)

    def last_outputs(n, _):
        finish(1 - n)
        return 0

    lax.fori_loop(0, 2, last_outputs, 0)

    def drain(h, _):
        to_partner(h).wait_send()
        forward(h).wait_send()

        @pl.when(h != z)
        def _():
            to_owner(h).wait_send()
            back(h, z).wait_send()

        return 0

    lax.fori_loop(0, HEADS, drain, 0)

    def drain_totals(other, _):
        to_seg(other).wait_send()
        return 0

    lax.fori_loop(seg + 1, NSEG, drain_totals, 0)


def shards(queries, keys, values, log_decay, gain):
    tokens = queries.shape[0]
    blocks = tokens // BLOCK
    heads = (HEADS, tokens, HD)
    vmem, dma = pltpu.VMEM, pltpu.SemaphoreType.DMA
    scratch = [
        vmem(heads, BF16), vmem(heads, BF16), vmem(heads, BF16),
        vmem((HEADS, tokens), F32), vmem((HEADS, 1, HD), F32),
        vmem((HEADS, 5, tokens), F32), vmem((2, TILE, TILE), F32), vmem((HEADS, blocks + 1, HD), F32),
        vmem((HEADS, blocks - 1, HD, HD), F32), vmem(heads, F32), vmem(heads, F32),
        vmem((HEADS, MSG, HD), F32), vmem((HEADS, MSG, HD), F32),
        vmem((NZ, SLAB, HD), F32), vmem((NZ, SLAB, HD), F32),
        vmem((NZ, HALF, HD), F32), vmem((NZ, 8, HD), F32),
        vmem((SLAB, HD), F32), vmem((NSEG, SLAB, HD), F32),
        vmem((NZ, HALF, HD), F32), vmem((HEADS, HD, HD), F32),
        dma((HEADS,)), dma((HEADS,)), dma((HEADS,)), dma((2,)),
        dma((HEADS,)), dma((HEADS,)), dma((NZ,)), dma((NZ,)),
        dma((NSEG,)), dma((NSEG,)), dma((NZ,)), dma((NZ,)), dma((HEADS,)), dma((HEADS,)),
        pltpu.SemaphoreType.REGULAR((2,)),
    ]
    operands = (queries, keys, values, log_decay, gain.reshape(HEADS, 1, HD))
    operands = [pltpu.with_memory_space_constraint(a, pltpu.HBM) for a in operands]
    return pl.pallas_call(
        kernel,
        out_shape=jax.ShapeDtypeStruct(queries.shape, BF16),
        in_specs=[pl.BlockSpec(memory_space=pltpu.HBM)] * 5,
        out_specs=pl.BlockSpec(memory_space=pltpu.VMEM),
        scratch_shapes=scratch,
        compiler_params=pltpu.CompilerParams(
            collective_id=0, has_side_effects=True, vmem_limit_bytes=48 * 1024 * 1024
        ),
        cost_estimate=pl.CostEstimate(flops=4 * 10**9, bytes_accessed=13 * 10**6, transcendentals=2 * 10**6),
    )(*operands)


def solution(mesh):
    in_specs = (
        P(("seg", "ctx"), None),
        P(("seg", "ctx"), None),
        P(("seg", "ctx"), None),
        P(None, ("seg", "ctx")),
        P(),
    )
    out_specs = P(("seg", "ctx"), None)
    return jax.shard_map(shards, mesh=mesh, in_specs=in_specs, out_specs=out_specs, check_vma=False)
```
